256 devices in a mesh: band: 4 (over y_lo, core), fft: 64 (over x, z, y_hi).
Axes of the slice: x: 4, y: 4 (y_hi: 2, y_lo: 2; y = y_hi * 2 + y_lo), z: 8, core: 2. Of those that a mesh axis runs over, the one named last changes fastest.
Arguments:
- receiving: float32 [16, 128, 128, 128], P('band', 'fft'), may hold values from -6 to 6
- occupied: float32 [4, 128, 128, 128], P('band', 'fft'), may hold values from -6 to 6
- coulomb: float32 [128, 128, 128], P(None, 'fft'), may hold values from 0.06 to 2.5, as said below
- pair_list: int32 [16, 4], P('band'), may hold values 0 or 1
Outputs:
- exchanged: float32 [16, 128, 128, 128], P('band', 'fft')
The draws below stay inside these ranges and needn't reach their ends.
Inputs may be any that keep to these rules, and one draw needn't show every extreme that they name: coulomb at indices (a, b, c) equals coulomb at ((-a) mod 128, (-b) mod 128, (-c) mod 128).
All inputs are finite; a program needn't handle non-finite values. No bound on the sum of `pair_list` on one device may be relied on, other than what follows from the above.
Results may differ from the reference program's by a relative error of at most 0.00013.
Values sent between devices are 32-bit elements; how exact they have to be, the bound alone decides.
No kernel may reach another device: no remote copies, remote signals or barrier semaphores. Data moves between devices by JAX's collectives and lax.ppermute only.
A program may use at most 64 MiB of HBM per device.

```python
import jax
import jax.numpy as jnp
from jax import lax

GRID = 128
RECV = 16
OCC = 4


def mirror(values):
    for dimension in range(3):
        values = jnp.roll(jnp.flip(values, dimension), 1, dimension)
    return values


def draw_coulomb(key, part):
    key = jax.random.fold_in(key, 7)
    roughness = jax.random.uniform(key, (GRID, GRID, GRID), jnp.float32, -1.0, 1.0)
    symmetric = roughness + mirror(roughness)
    return 0.4 * jnp.exp(0.9 * symmetric)


def place_ends(entries, stream_key, least, largest):
    longest = entries.shape.index(max(entries.shape))
    spots = []
    for shift in (0, 1):
        where = [jax.random.randint(jax.random.fold_in(stream_key, axis), (), 0, length) for axis, length in enumerate(entries.shape)]
        where[longest] = (where[longest] + shift) % entries.shape[longest]
        spots.append(tuple(where))
    return entries.at[spots[0]].set(least).at[spots[1]].set(largest)


def block_scale(stream_key, shape, split, low, top_value):
    level = 1.0
    for axis_at, blocks in split:
        draws = jax.random.uniform(jax.random.fold_in(jax.random.fold_in(stream_key, 6), axis_at), (blocks,), jnp.float32, low / len(split), top_value / len(split))
        level = level * jnp.repeat(jnp.exp(draws), shape[axis_at] // blocks).reshape((-1,) + (1,) * (len(shape) - 1 - axis_at))
    return level


def centred(stream_key, shape, width, bound, cuts=(), kind=jnp.bfloat16):
    values = jax.random.normal(stream_key, shape, jnp.float32) * width
    if len(cuts) > 0:
        values = block_scale(stream_key, shape, cuts, -0.22, 0.18) * values
    return jnp.clip(values, min=-bound, max=bound).astype(kind)


def setup_inputs(seed: int = 0) -> dict:
    splits = jax.random.split(jax.random.key(seed), 5)
    receiving = centred(splits[0], (RECV, GRID, GRID, GRID), 1.0, 6.0, ((0, 4), (1, 64)), jnp.float32)
    occupied = centred(splits[1], (OCC, GRID, GRID, GRID), 1.0, 6.0, ((0, 4), (1, 64)), jnp.float32)
    coulomb = draw_coulomb(jax.random.fold_in(splits[4], 71), 0)
    pair_list = place_ends((jax.random.randint(splits[3], (RECV, OCC), 0, 4) < 3).astype(jnp.int32), jax.random.fold_in(splits[3], 1), 0, 1)
    return {"receiving": receiving, "occupied": occupied, "coulomb": coulomb, "pair_list": pair_list}


def reference(receiving, occupied, coulomb, pair_list):
    weights = pair_list.astype(jnp.float32)

    def exchange_one(operands):
        orbital, row_weights = operands
        accumulated = jnp.zeros(orbital.shape, jnp.float32)
        for orbital_index in range(OCC):
            partner = occupied[orbital_index]
            spectrum = jnp.fft.fftn(orbital * partner)
            potential = jnp.real(jnp.fft.ifftn(coulomb * spectrum))
            accumulated = accumulated + row_weights[orbital_index] * partner * potential
        return -0.25 * accumulated

    return lax.map(exchange_one, (receiving, weights))
```

```python
import numpy as np

import jax
import jax.numpy as jnp
from jax import lax
from jax.experimental import pallas as pl
from jax.experimental.pallas import tpu as pltpu
from jax.sharding import PartitionSpec as P

grid = 128
devices = 64
planes = grid // devices
mixing = 0.25


def rotation():
    angles = 2.0 * np.pi / grid * (np.arange(grid)[:, None] * np.arange(grid)[None, :] % grid)
    return np.cos(angles), np.sin(angles)


def halves(matrix):
    high = matrix.astype(jnp.bfloat16)
    low = (matrix - high.astype(np.float64)).astype(jnp.bfloat16)
    return np.stack([high, low])


def tables():
    cos, sin = rotation()
    forward = np.block([[cos, -sin], [sin, cos]])
    inverse = np.block([[cos, sin], [-sin, cos]])
    part, row = np.divmod(np.arange(2 * grid), grid)
    spread = part * grid + row % devices * planes + row // devices
    woven = np.arange(2 * grid) % 2 * grid + np.arange(2 * grid) // 2
    return {
        "z": halves(forward),
        "y": halves(forward.T[spread]),
        "x": halves(forward.T[:, woven]),
        "x_back": halves(inverse.T[woven]),
        "y_back": halves(inverse.T[:, spread]),
        "z_back": halves(inverse),
    }


def split(value):
    high = value.astype(jnp.bfloat16)
    low = (value - high.astype(jnp.float32)).astype(jnp.bfloat16)
    return high, low


def dot(left, right):
    return jnp.dot(left, right, preferred_element_type=jnp.float32)


def right_transform(value, table):
    high, low = split(value)
    return dot(high, table[0]) + (dot(low, table[0]) + dot(high, table[1]))


def left_transform(table, value):
    high, low = split(value)
    return dot(table[0], high) + (dot(table[0], low) + dot(table[1], high))


def stack_parts(value):
    top, bottom = value[:grid], value[grid:]
    return jnp.concatenate(
        [
            jnp.concatenate([top[:, :grid], bottom[:, :grid]], 1),
            jnp.concatenate([top[:, grid:], bottom[:, grid:]], 1),
        ],
        0,
    )


def chunk_row(plane, part, field, fields):
    return ((plane * 2 + part) * fields + field) * planes


def forward_kernel(recv_ref, occ_ref, z_ref, y_ref, out_ref):
    received = recv_ref.shape[0]
    fields = 2 * received
    chunk = planes * 2 * fields * planes
    for plane in range(planes):
        for orbital in range(received):
            density = recv_ref[orbital, plane]
            products = [density * occ_ref[j, plane] for j in range(4)]
            value = jnp.concatenate(
                [
                    jnp.concatenate(products[:2], 1),
                    jnp.concatenate(products[2:], 1),
                ],
                0,
            )
            value = left_transform(y_ref, stack_parts(right_transform(value, z_ref)))
            for part in range(2):
                for field in range(2):
                    start = chunk_row(plane, part, orbital * 2 + field, fields)
                    for place in range(planes):
                        row = part * grid + place * devices
                        out_ref[pl.ds(start + place, devices, stride=chunk), :] = value[
                            row : row + devices, field * grid : (field + 1) * grid
                        ]


def filter_kernel(spec_ref, coulomb_ref, x_ref, back_ref, out_ref):
    columns = spec_ref.shape[0] // (2 * grid)
    for pair in range(columns // (2 * planes)):
        for place in range(planes):
            starts = [(pair * 2 + field) * planes + place for field in range(2)]
            value = jnp.concatenate(
                [spec_ref[pl.ds(start, 2 * grid, stride=columns), :] for start in starts], 1
            )
            kernel = coulomb_ref[:, place, :]
            kernel = jnp.concatenate([kernel, kernel], 1)
            kernel = jnp.concatenate([kernel, kernel], 0)
            value = left_transform(back_ref, left_transform(x_ref, value) * kernel)
            for field, start in enumerate(starts):
                out_ref[pl.ds(start, 2 * grid, stride=columns), :] = value[
                    :, field * grid : (field + 1) * grid
                ]


def inverse_kernel(weights_ref, spec_ref, occ_ref, y_ref, z_ref, out_ref):
    received = out_ref.shape[0]
    fields = 2 * received
    chunk = planes * 2 * fields * planes
    for plane in range(planes):
        for orbital in range(received):
            value = jnp.concatenate(
                [
                    jnp.concatenate(
                        [
                            spec_ref[
                                pl.ds(
                                    chunk_row(plane, part, orbital * 2 + field, fields) + place,
                                    devices,
                                    stride=chunk,
                                ),
                                :,
                            ]
                            for field in range(2)
                        ],
                        1,
                    )
                    for part in range(2)
                    for place in range(planes)
                ],
                0,
            )
            value = right_transform(stack_parts(left_transform(y_ref, value)), z_ref)
            total = jnp.zeros((grid, grid), jnp.float32)
            for j in range(4):
                field, part = divmod(j, 2)
                potential = value[
                    field * grid : (field + 1) * grid, part * grid : (part + 1) * grid
                ]
                total += weights_ref[orbital, j] * occ_ref[j, plane] * potential
            out_ref[orbital, plane] = total


vmem = pl.BlockSpec(memory_space=pltpu.VMEM)
smem = pl.BlockSpec(memory_space=pltpu.SMEM)


def call(kernel, shape, in_specs, *operands):
    return pl.pallas_call(
        kernel,
        out_shape=jax.ShapeDtypeStruct(shape, jnp.float32),
        in_specs=in_specs,
        out_specs=vmem,
        compiler_params=pltpu.CompilerParams(vmem_limit_bytes=40 * 1024 * 1024),
    )(*operands)


def on_device(receiving, occupied, coulomb, pair_list):
    table = tables()
    orbitals = lax.all_gather(occupied, "band", axis=0, tiled=True)
    weights = pair_list.astype(jnp.float32) * (-mixing / grid**3)
    rows = planes * 2 * 2 * receiving.shape[0] * planes
    spectrum = call(
        forward_kernel,
        (devices * rows, grid),
        [vmem] * 4,
        receiving,
        orbitals,
        table["z"],
        table["y"],
    )
    spectrum = lax.all_to_all(
        spectrum.reshape(devices, rows, grid), "fft", split_axis=0, concat_axis=0, tiled=True
    ).reshape(devices * rows, grid)
    spectrum = call(
        filter_kernel,
        spectrum.shape,
        [vmem] * 4,
        spectrum,
        coulomb,
        table["x"],
        table["x_back"],
    )
    spectrum = lax.all_to_all(
        spectrum.reshape(devices, rows, grid), "fft", split_axis=0, concat_axis=0, tiled=True
    ).reshape(devices * rows, grid)
    return call(
        inverse_kernel,
        receiving.shape,
        [smem] + [vmem] * 4,
        weights,
        spectrum,
        orbitals,
        table["y_back"],
        table["z_back"],
    )


def solution(mesh):
    in_specs = (
        P("band", "fft", None, None),
        P("band", "fft", None, None),
        P(None, "fft", None),
        P("band", None),
    )
    out_specs = P("band", "fft", None, None)
    return jax.shard_map(
        on_device, mesh=mesh, in_specs=in_specs, out_specs=out_specs, check_vma=False
    )
```

```python
import functools

import numpy as np

import jax
import jax.numpy as jnp
from jax import lax
from jax.experimental import pallas as pl
from jax.experimental.pallas import tpu as pltpu
from jax.sharding import PartitionSpec as P

grid = 128
mixing = 0.25
slabs = 4
members = 16
run = 2
planes = slabs * run
fields = 2
columns = fields * planes
chunk = planes * 2 * columns
groups = [
    [x * 16 + slab * 4 + rest for x in range(4) for rest in range(4)] for slab in range(slabs)
]


def slab_steps(step):
    return [(index, index ^ (step * 4)) for index in range(64)]


def halves(matrix):
    high = matrix.astype(jnp.bfloat16)
    low = (matrix - high.astype(np.float64)).astype(jnp.bfloat16)
    return np.stack([high, low])


def position(member, plane):
    return member // 4 * 32 + plane // run * 8 + member % 4 * run + plane % run


def tables():
    angles = 2.0 * np.pi / grid * (np.arange(grid)[:, None] * np.arange(grid)[None, :] % grid)
    cos, sin = np.cos(angles), np.sin(angles)
    forward = np.block([[cos, -sin], [sin, cos]])
    inverse = np.block([[cos, sin], [-sin, cos]])
    part, rest = np.divmod(np.arange(2 * grid), grid)
    spread = part * grid + position(rest % members, rest // members)
    rest, part = np.divmod(np.arange(2 * grid), 2)
    woven = part * grid + position(rest // planes, rest % planes)
    return {
        "z": halves(forward),
        "y": halves(forward.T[spread]),
        "x": halves(forward.T[:, woven]),
        "x_back": halves(inverse.T[woven]),
        "y_back": halves(inverse.T[:, spread]),
        "z_back": halves(inverse),
    }


def split(value):
    high = value.astype(jnp.bfloat16)
    low = (value - high.astype(jnp.float32)).astype(jnp.bfloat16)
    return high, low


def dot(left, right):
    return jnp.dot(left, right, preferred_element_type=jnp.float32)


def right_transform(value, table):
    high, low = split(value)
    return dot(high, table[0]) + (dot(low, table[0]) + dot(high, table[1]))


def left_transform(table, value):
    high, low = split(value)
    return dot(table[0], high) + (dot(table[0], low) + dot(table[1], high))


def stack_parts(value):
    top, bottom = value[:grid], value[grid:]
    return jnp.concatenate(
        [
            jnp.concatenate([top[:, :grid], bottom[:, :grid]], 1),
            jnp.concatenate([top[:, grid:], bottom[:, grid:]], 1),
        ],
        0,
    )


def member_rows(plane, part, field, place):
    start = pl.multiple_of(plane * (2 * columns), 2 * columns)
    return pl.ds(start + (part * columns + field * planes + place), members, stride=chunk)


def forward_kernel(slab_ref, r0, r1, r2, r3, occ_ref, z_ref, y_ref, out_ref):
    for step, recv_ref in enumerate((r0, r1, r2, r3)):
        for inner in range(run):
            plane = (slab_ref[0] ^ step) * run + inner
            density = recv_ref[inner]
            products = [density * occ_ref[j, step, inner] for j in range(4)]
            value = jnp.concatenate(
                [
                    jnp.concatenate(products[:2], 1),
                    jnp.concatenate(products[2:], 1),
                ],
                0,
            )
            value = left_transform(y_ref, stack_parts(right_transform(value, z_ref)))
            for part in range(2):
                for field in range(fields):
                    for place in range(planes):
                        row = part * grid + place * members
                        out_ref[member_rows(plane, part, field, place), :] = value[
                            row : row + members, field * grid : (field + 1) * grid
                        ]


def filter_kernel(slab_ref, spec_ref, c0, c1, c2, c3, x_ref, back_ref, out_ref):
    for step, coulomb_ref in enumerate((c0, c1, c2, c3)):
        for inner in range(run):
            place = (slab_ref[0] ^ step) * run + inner
            rows = [
                pl.ds(field * planes + place, 2 * grid, stride=columns)
                for field in range(fields)
            ]
            value = jnp.concatenate([spec_ref[row, :] for row in rows], 1)
            kernel = coulomb_ref[:, inner, :]
            kernel = jnp.concatenate([kernel, kernel], 1)
            kernel = jnp.concatenate([kernel, kernel], 0)
            value = left_transform(back_ref, left_transform(x_ref, value) * kernel)
            for field, row in enumerate(rows):
                out_ref[row, :] = value[:, field * grid : (field + 1) * grid]


def inverse_kernel(slab_ref, weights_ref, spec_ref, occ_ref, y_ref, z_ref, o0, o1, o2, o3):
    slab = slab_ref[0]
    for step, out_ref in enumerate((o0, o1, o2, o3)):
        for inner in range(run):
            plane = (slab ^ step) * run + inner
            value = jnp.concatenate(
                [
                    jnp.concatenate(
                        [
                            spec_ref[member_rows(plane, part, field, place), :]
                            for field in range(fields)
                        ],
                        1,
                    )
                    for part in range(2)
                    for place in range(planes)
                ],
                0,
            )
            value = right_transform(stack_parts(left_transform(y_ref, value)), z_ref)
            total = jnp.zeros((grid, grid), jnp.float32)
            for j in range(4):
                field, part = divmod(j, 2)
                potential = value[
                    field * grid : (field + 1) * grid, part * grid : (part + 1) * grid
                ]
                total += weights_ref[slab, j] * occ_ref[j, step, inner] * potential
            out_ref[inner] = total


def collect_kernel(slab_ref, b0, b1, b2, b3, out_ref):
    for step, block_ref in enumerate((b0, b1, b2, b3)):
        out_ref[slab_ref[0] ^ step] = block_ref[...]


vmem = pl.BlockSpec(memory_space=pltpu.VMEM)
smem = pl.BlockSpec(memory_space=pltpu.SMEM)


def call(kernel, shapes, scalars, *operands):
    shapes = jax.tree.map(
        lambda shape: jax.ShapeDtypeStruct(shape, jnp.float32),
        shapes,
        is_leaf=lambda node: isinstance(node[0], int),
    )
    return pl.pallas_call(
        kernel,
        out_shape=shapes,
        in_specs=[smem] * len(scalars) + [vmem] * len(operands),
        out_specs=jax.tree.map(lambda shape: vmem, shapes),
        compiler_params=pltpu.CompilerParams(vmem_limit_bytes=40 * 1024 * 1024),
    )(*scalars, *operands)


def exchange(block, step):
    if step == 0:
        return block
    return lax.ppermute(block, "fft", slab_steps(step))


def regroup(spectrum):
    return lax.all_to_all(
        spectrum.reshape(members, chunk, grid),
        "fft",
        split_axis=0,
        concat_axis=0,
        axis_index_groups=groups,
        tiled=True,
    ).reshape(spectrum.shape)


def on_device(receiving, occupied, coulomb, pair_list):
    table = tables()
    slab = lax.axis_index("fft") // 4 % slabs
    slab_word = slab.astype(jnp.int32).reshape(1)
    weights = pair_list.astype(jnp.float32) * (-mixing / grid**3)

    orbitals = jnp.concatenate([exchange(occupied, step) for step in range(slabs)], 0)
    orbitals = lax.all_gather(orbitals[None], "band", axis=0, tiled=True)
    received = [
        exchange(lax.dynamic_index_in_dim(receiving, slab ^ step, 0, keepdims=False), step)
        for step in range(slabs)
    ]
    kernels = [exchange(coulomb, step) for step in range(slabs)]

    spectrum = call(
        forward_kernel,
        (members * chunk, grid),
        [slab_word],
        *received,
        orbitals,
        table["z"],
        table["y"],
    )
    spectrum = regroup(spectrum)
    spectrum = call(
        filter_kernel,
        spectrum.shape,
        [slab_word],
        spectrum,
        *kernels,
        table["x"],
        table["x_back"],
    )
    spectrum = regroup(spectrum)
    blocks = call(
        inverse_kernel,
        [(run, grid, grid)] * slabs,
        [slab_word, weights],
        spectrum,
        orbitals,
        table["y_back"],
        table["z_back"],
    )
    blocks = [exchange(block, step) for step, block in enumerate(blocks)]
    return call(collect_kernel, receiving.shape, [slab_word], *blocks)


def solution(mesh):
    in_specs = (
        P("band", "fft", None, None),
        P("band", "fft", None, None),
        P(None, "fft", None),
        P("band", None),
    )
    out_specs = P("band", "fft", None, None)
    return jax.shard_map(
        on_device, mesh=mesh, in_specs=in_specs, out_specs=out_specs, check_vma=False
    )
```

```python
import functools

import numpy as np

import jax
import jax.numpy as jnp
from jax import lax
from jax.experimental import pallas as pl
from jax.experimental.pallas import tpu as pltpu
from jax.sharding import PartitionSpec as P

grid = 128
mixing = 0.25
devices = 64
planes = grid // devices
orbitals = 4
pairs = orbitals * orbitals
field_counts = (4, 5, 6, 7, 8)


def halves(matrix):
    high = matrix.astype(jnp.bfloat16)
    low = (matrix - high.astype(np.float64)).astype(jnp.bfloat16)
    return np.stack([high, low])


def tables():
    angles = 2.0 * np.pi / grid * (np.arange(grid)[:, None] * np.arange(grid)[None, :] % grid)
    cos, sin = np.cos(angles), np.sin(angles)
    forward = np.block([[cos, -sin], [sin, cos]])
    inverse = np.block([[cos, sin], [-sin, cos]])
    part, row = np.divmod(np.arange(2 * grid), grid)
    spread = part * grid + row % devices * planes + row // devices
    woven = np.arange(2 * grid) % 2 * grid + np.arange(2 * grid) // 2
    return {
        "z": halves(forward),
        "y": halves(forward.T[spread]),
        "x": halves(forward.T[:, woven]),
        "x_back": halves(inverse.T[woven]),
        "y_back": halves(inverse.T[:, spread]),
        "z_back": halves(inverse),
    }


def split(value):
    high = value.astype(jnp.bfloat16)
    low = (value - high.astype(jnp.float32)).astype(jnp.bfloat16)
    return high, low


def dot(left, right):
    return jnp.dot(left, right, preferred_element_type=jnp.float32)


def right_transform(value, table):
    high, low = split(value)
    return dot(high, table[0]) + (dot(low, table[0]) + dot(high, table[1]))


def left_transform(table, value):
    high, low = split(value)
    return dot(table[0], high) + (dot(table[0], low) + dot(table[1], high))


def stack_parts(value):
    top, bottom = value[:grid], value[grid:]
    return jnp.concatenate(
        [
            jnp.concatenate([top[:, :grid], bottom[:, :grid]], 1),
            jnp.concatenate([top[:, grid:], bottom[:, grid:]], 1),
        ],
        0,
    )


def chunk_rows(fields):
    return planes * 2 * fields * planes


def device_rows(fields, plane, part, field, place):
    start = ((plane * 2 + part) * fields + field) * planes + place
    return pl.ds(start, devices, stride=chunk_rows(fields))


def line_rows(fields, field, place):
    return pl.ds(field * planes + place, 2 * grid, stride=fields * planes)


def list_pairs(pairs_ref, order_ref):
    for index in range(pairs):
        order_ref[index] = 0
    count = jnp.int32(0)
    for index in range(pairs):
        order_ref[count] = index
        count += (pairs_ref[index // orbitals, index % orbitals] != 0).astype(jnp.int32)
    return count


def forward_kernel(
    fields, pairs_ref, recv_any, occ_any, z_any, y_any, out_ref, recv_ref, occ_ref, z_ref, y_ref, order_ref, sem
):
    copies = [
        pltpu.make_async_copy(source, target, sem.at[index])
        for index, (source, target) in enumerate(
            [(recv_any, recv_ref), (occ_any, occ_ref), (z_any, z_ref), (y_any, y_ref)]
        )
    ]
    for copy in copies:
        copy.start()
    list_pairs(pairs_ref, order_ref)
    for copy in copies:
        copy.wait()
    for field in range(fields):
        couple = [order_ref[2 * field + part] for part in range(2)]
        value = jnp.concatenate(
            [
                jnp.concatenate(
                    [
                        recv_ref[pair // orbitals, plane] * occ_ref[pair % orbitals, plane]
                        for pair in couple
                    ],
                    1,
                )
                for plane in range(planes)
            ],
            0,
        )
        value = left_transform(y_ref, stack_parts(right_transform(value, z_ref)))
        for part in range(2):
            for place in range(planes):
                row = part * grid + place * devices
                for plane in range(planes):
                    out_ref[device_rows(fields, plane, part, field, place), :] = value[
                        row : row + devices, plane * grid : (plane + 1) * grid
                    ]


def filter_kernel(fields, spec_ref, coulomb_ref, x_ref, back_ref, out_ref):
    kernel = jnp.concatenate([coulomb_ref[:, place, :] for place in range(planes)], 1)
    kernel = jnp.concatenate([kernel, kernel], 0)
    for field in range(fields):
        rows = [line_rows(fields, field, place) for place in range(planes)]
        value = jnp.concatenate([spec_ref[row, :] for row in rows], 1)
        value = left_transform(back_ref, left_transform(x_ref, value) * kernel)
        for place, row in enumerate(rows):
            out_ref[row, :] = value[:, place * grid : (place + 1) * grid]


def inverse_kernel(
    fields, pairs_ref, weights_ref, spec_ref, occ_ref, y_ref, z_ref, out_ref, order_ref
):
    count = list_pairs(pairs_ref, order_ref)
    out_ref[...] = jnp.zeros_like(out_ref)
    for field in range(fields):
        value = jnp.concatenate(
            [
                jnp.concatenate(
                    [
                        spec_ref[device_rows(fields, plane, part, field, place), :]
                        for plane in range(planes)
                    ],
                    1,
                )
                for part in range(2)
                for place in range(planes)
            ],
            0,
        )
        value = right_transform(stack_parts(left_transform(y_ref, value)), z_ref)
        for part in range(2):
            pair = order_ref[2 * field + part]
            received, occupied = pair // orbitals, pair % orbitals
            weight = jnp.where(2 * field + part < count, weights_ref[received, occupied], 0.0)
            for plane in range(planes):
                potential = value[
                    plane * grid : (plane + 1) * grid, part * grid : (part + 1) * grid
                ]
                out_ref[received, plane] += weight * occ_ref[occupied, plane] * potential


vmem = pl.BlockSpec(memory_space=pltpu.VMEM)
smem = pl.BlockSpec(memory_space=pltpu.SMEM)
anywhere = pl.BlockSpec(memory_space=pl.ANY)


def call(kernel, shape, in_specs, *operands, scratch=()):
    return pl.pallas_call(
        kernel,
        out_shape=jax.ShapeDtypeStruct(shape, jnp.float32),
        in_specs=in_specs,
        out_specs=vmem,
        scratch_shapes=scratch,
        compiler_params=pltpu.CompilerParams(vmem_limit_bytes=24 * 1024 * 1024),
    )(*operands)


def regroup(spectrum):
    return lax.all_to_all(
        spectrum.reshape(devices, -1, grid), "fft", split_axis=0, concat_axis=0, tiled=True
    ).reshape(spectrum.shape)


def exchange(fields, receiving, partners, coulomb, pair_list, weights):
    table = tables()
    order = pltpu.SMEM((pairs,), jnp.int32)
    spectrum = call(
        functools.partial(forward_kernel, fields),
        (devices * chunk_rows(fields), grid),
        [smem] + [anywhere] * 4,
        pair_list,
        receiving,
        partners,
        table["z"],
        table["y"],
        scratch=[
            pltpu.VMEM(receiving.shape, jnp.float32),
            pltpu.VMEM(partners.shape, jnp.float32),
            pltpu.VMEM(table["z"].shape, jnp.bfloat16),
            pltpu.VMEM(table["y"].shape, jnp.bfloat16),
            order,
            pltpu.SemaphoreType.DMA((4,)),
        ],
    )
    spectrum = regroup(spectrum)
    spectrum = call(
        functools.partial(filter_kernel, fields),
        spectrum.shape,
        [vmem] * 4,
        spectrum,
        coulomb,
        table["x"],
        table["x_back"],
    )
    spectrum = regroup(spectrum)
    return call(
        functools.partial(inverse_kernel, fields),
        receiving.shape,
        [smem] * 2 + [vmem] * 4,
        pair_list,
        weights,
        spectrum,
        partners,
        table["y_back"],
        table["z_back"],
        scratch=[order],
    )


def on_device(receiving, occupied, coulomb, pair_list):
    partners = lax.all_gather(occupied, "band", axis=0, tiled=True)
    weights = pair_list.astype(jnp.float32) * (-mixing / grid**3)
    live = jnp.sum((pair_list != 0).astype(jnp.int32))
    chosen = jnp.maximum((live + 1) // 2 - field_counts[0], 0)
    return lax.switch(
        chosen,
        [functools.partial(exchange, fields) for fields in field_counts],
        receiving,
        partners,
        coulomb,
        pair_list,
        weights,
    )


def solution(mesh):
    in_specs = (
        P("band", "fft", None, None),
        P("band", "fft", None, None),
        P(None, "fft", None),
        P("band", None),
    )
    out_specs = P("band", "fft", None, None)
    return jax.shard_map(
        on_device, mesh=mesh, in_specs=in_specs, out_specs=out_specs, check_vma=False
    )
```

```python
import functools

import numpy as np

import jax
import jax.numpy as jnp
from jax import lax
from jax.experimental import pallas as pl
from jax.experimental.pallas import tpu as pltpu
from jax.sharding import PartitionSpec as P

grid = 128
mixing = 0.25
devices = 64
planes = grid // devices
orbitals = 4
pairs = orbitals * orbitals
field_counts = (4, 5, 6, 7, 8)


def halves(matrix):
    high = matrix.astype(jnp.bfloat16)
    low = (matrix - high.astype(np.float64)).astype(jnp.bfloat16)
    return np.stack([high, low])


def tables():
    angles = 2.0 * np.pi / grid * (np.arange(grid)[:, None] * np.arange(grid)[None, :] % grid)
    cos, sin = np.cos(angles), np.sin(angles)
    forward = np.block([[cos, -sin], [sin, cos]])
    inverse = np.block([[cos, sin], [-sin, cos]])
    part, row = np.divmod(np.arange(2 * grid), grid)
    spread = part * grid + row % devices * planes + row // devices
    woven = np.arange(2 * grid) % 2 * grid + np.arange(2 * grid) // 2
    return {
        "z": halves(forward),
        "y": halves(forward.T[spread]),
        "x": halves(forward.T[:, woven]),
        "x_back": halves(inverse.T[woven]),
        "y_back": halves(inverse.T[:, spread]),
        "z_back": halves(inverse),
    }


def split(value):
    high = value.astype(jnp.bfloat16)
    low = (value - high.astype(jnp.float32)).astype(jnp.bfloat16)
    return high, low


def dot(left, right):
    return jnp.dot(left, right, preferred_element_type=jnp.float32)


def right_transform(value, table):
    high, low = split(value)
    return dot(high, table[0]) + (dot(low, table[0]) + dot(high, table[1]))


def left_transform(table, value):
    high, low = split(value)
    return dot(table[0], high) + (dot(table[0], low) + dot(table[1], high))


def stack_parts(value):
    top, bottom = value[:grid], value[grid:]
    return jnp.concatenate(
        [
            jnp.concatenate([top[:, :grid], bottom[:, :grid]], 1),
            jnp.concatenate([top[:, grid:], bottom[:, grid:]], 1),
        ],
        0,
    )


def chunk_rows(fields):
    return planes * 2 * fields * planes


def device_rows(fields, plane, part, field, place):
    start = ((plane * 2 + part) * fields + field) * planes + place
    return pl.ds(start, devices, stride=chunk_rows(fields))


def line_rows(fields, field, place):
    return pl.ds(field * planes + place, 2 * grid, stride=fields * planes)


def list_pairs(pairs_ref, order_ref):
    for index in range(pairs):
        order_ref[index] = 0
    count = jnp.int32(0)
    for index in range(pairs):
        order_ref[count] = index
        count += (pairs_ref[index // orbitals, index % orbitals] != 0).astype(jnp.int32)
    return count


def each_field(fields):
    def run(body):
        @pl.loop(0, fields // 2)
        def _(couple):
            body(2 * couple)
            body(2 * couple + 1)

        if fields % 2:
            body(fields - 1)

    return run


def forward_kernel(
    fields, pairs_ref, recv_any, occ_any, z_any, y_any, out_ref, recv_ref, occ_ref, z_ref, y_ref, order_ref, sem
):
    copies = [
        pltpu.make_async_copy(source, target, sem.at[index])
        for index, (source, target) in enumerate(
            [(recv_any, recv_ref), (occ_any, occ_ref), (z_any, z_ref), (y_any, y_ref)]
        )
    ]
    for copy in copies:
        copy.start()
    list_pairs(pairs_ref, order_ref)
    for copy in copies:
        copy.wait()

    @each_field(fields)
    def _(field):
        couple = [order_ref[2 * field + part] for part in range(2)]
        value = jnp.concatenate(
            [
                jnp.concatenate(
                    [
                        recv_ref[pair // orbitals, plane] * occ_ref[pair % orbitals, plane]
                        for pair in couple
                    ],
                    1,
                )
                for plane in range(planes)
            ],
            0,
        )
        value = left_transform(y_ref, stack_parts(right_transform(value, z_ref)))
        for part in range(2):
            for place in range(planes):
                row = part * grid + place * devices
                for plane in range(planes):
                    out_ref[device_rows(fields, plane, part, field, place), :] = value[
                        row : row + devices, plane * grid : (plane + 1) * grid
                    ]


def filter_kernel(fields, spec_ref, coulomb_ref, x_ref, back_ref, out_ref):
    kernel = jnp.concatenate([coulomb_ref[:, place, :] for place in range(planes)], 1)
    kernel = jnp.concatenate([kernel, kernel], 0)

    @each_field(fields)
    def _(field):
        rows = [line_rows(fields, field, place) for place in range(planes)]
        value = jnp.concatenate([spec_ref[row, :] for row in rows], 1)
        value = left_transform(back_ref, left_transform(x_ref, value) * kernel)
        for place, row in enumerate(rows):
            out_ref[row, :] = value[:, place * grid : (place + 1) * grid]


def inverse_kernel(
    fields, pairs_ref, weights_ref, spec_ref, occ_ref, y_ref, z_ref, out_ref, order_ref
):
    count = list_pairs(pairs_ref, order_ref)
    out_ref[...] = jnp.zeros_like(out_ref)

    @each_field(fields)
    def _(field):
        value = jnp.concatenate(
            [
                jnp.concatenate(
                    [
                        spec_ref[device_rows(fields, plane, part, field, place), :]
                        for plane in range(planes)
                    ],
                    1,
                )
                for part in range(2)
                for place in range(planes)
            ],
            0,
        )
        value = right_transform(stack_parts(left_transform(y_ref, value)), z_ref)
        for part in range(2):
            pair = order_ref[2 * field + part]
            received, occupied = pair // orbitals, pair % orbitals
            weight = jnp.where(2 * field + part < count, weights_ref[received, occupied], 0.0)
            for plane in range(planes):
                potential = value[
                    plane * grid : (plane + 1) * grid, part * grid : (part + 1) * grid
                ]
                out_ref[received, plane] += weight * occ_ref[occupied, plane] * potential


vmem = pl.BlockSpec(memory_space=pltpu.VMEM)
smem = pl.BlockSpec(memory_space=pltpu.SMEM)
anywhere = pl.BlockSpec(memory_space=pl.ANY)


def call(kernel, shape, in_specs, *operands, scratch=()):
    return pl.pallas_call(
        kernel,
        out_shape=jax.ShapeDtypeStruct(shape, jnp.float32),
        in_specs=in_specs,
        out_specs=vmem,
        scratch_shapes=scratch,
        compiler_params=pltpu.CompilerParams(vmem_limit_bytes=24 * 1024 * 1024),
    )(*operands)


def regroup(spectrum):
    return lax.all_to_all(
        spectrum.reshape(devices, -1, grid), "fft", split_axis=0, concat_axis=0, tiled=True
    ).reshape(spectrum.shape)


def exchange(fields, receiving, partners, coulomb, pair_list, weights, table):
    order = pltpu.SMEM((pairs,), jnp.int32)
    spectrum = call(
        functools.partial(forward_kernel, fields),
        (devices * chunk_rows(fields), grid),
        [smem] + [anywhere] * 4,
        pair_list,
        receiving,
        partners,
        table["z"],
        table["y"],
        scratch=[
            pltpu.VMEM(receiving.shape, jnp.float32),
            pltpu.VMEM(partners.shape, jnp.float32),
            pltpu.VMEM(table["z"].shape, jnp.bfloat16),
            pltpu.VMEM(table["y"].shape, jnp.bfloat16),
            order,
            pltpu.SemaphoreType.DMA((4,)),
        ],
    )
    spectrum = regroup(spectrum)
    spectrum = call(
        functools.partial(filter_kernel, fields),
        spectrum.shape,
        [vmem] * 4,
        spectrum,
        coulomb,
        table["x"],
        table["x_back"],
    )
    spectrum = regroup(spectrum)
    return call(
        functools.partial(inverse_kernel, fields),
        receiving.shape,
        [smem] * 2 + [vmem] * 4,
        pair_list,
        weights,
        spectrum,
        partners,
        table["y_back"],
        table["z_back"],
        scratch=[order],
    )


def on_device(receiving, occupied, coulomb, pair_list):
    partners = lax.all_gather(occupied, "band", axis=0, tiled=True)
    weights = pair_list.astype(jnp.float32) * (-mixing / grid**3)
    live = jnp.sum((pair_list != 0).astype(jnp.int32))
    chosen = jnp.maximum((live + 1) // 2 - field_counts[0], 0)
    return lax.switch(
        chosen,
        [functools.partial(exchange, fields) for fields in field_counts],
        receiving,
        partners,
        coulomb,
        pair_list,
        weights,
        lax.optimization_barrier(jax.tree.map(jnp.asarray, tables())),
    )


def solution(mesh):
    in_specs = (
        P("band", "fft", None, None),
        P("band", "fft", None, None),
        P(None, "fft", None),
        P("band", None),
    )
    out_specs = P("band", "fft", None, None)
    return jax.shard_map(
        on_device, mesh=mesh, in_specs=in_specs, out_specs=out_specs, check_vma=False
    )
```

```python
import functools

import numpy as np

import jax
import jax.numpy as jnp
from jax import lax
from jax.experimental import pallas as pl
from jax.experimental.pallas import tpu as pltpu
from jax.sharding import PartitionSpec as P

grid = 128
mixing = 0.25
devices = 64
planes = grid // devices
orbitals = 4
pairs = orbitals * orbitals
field_counts = (4, 5, 6, 7, 8)


def halves(matrix):
    high = matrix.astype(jnp.bfloat16)
    low = (matrix - high.astype(np.float64)).astype(jnp.bfloat16)
    return np.stack([high, low])


def tables():
    angles = 2.0 * np.pi / grid * (np.arange(grid)[:, None] * np.arange(grid)[None, :] % grid)
    cos, sin = np.cos(angles), np.sin(angles)
    forward = np.block([[cos, -sin], [sin, cos]])
    inverse = np.block([[cos, sin], [-sin, cos]])
    part, row = np.divmod(np.arange(2 * grid), grid)
    spread = part * grid + row % devices * planes + row // devices
    woven = np.arange(2 * grid) % 2 * grid + np.arange(2 * grid) // 2
    return {
        "z": halves(forward),
        "y": halves(forward.T[spread]),
        "x": halves(forward.T[:, woven]),
        "x_back": halves(inverse.T[woven]),
        "y_back": halves(inverse.T[:, spread]),
        "z_back": halves(inverse),
    }


def split(value):
    high = value.astype(jnp.bfloat16)
    low = (value - high.astype(jnp.float32)).astype(jnp.bfloat16)
    return high, low


def dot(left, right):
    return jnp.dot(left, right, preferred_element_type=jnp.float32)


def right_transform(value, table):
    high, low = split(value)
    return dot(high, table[0]) + (dot(low, table[0]) + dot(high, table[1]))


def left_transform(table, value):
    high, low = split(value)
    return dot(table[0], high) + (dot(table[0], low) + dot(table[1], high))


def stack_parts(value):
    top, bottom = value[:grid], value[grid:]
    return jnp.concatenate(
        [
            jnp.concatenate([top[:, :grid], bottom[:, :grid]], 1),
            jnp.concatenate([top[:, grid:], bottom[:, grid:]], 1),
        ],
        0,
    )


def chunk_rows(fields):
    return planes * 2 * fields * planes


def device_rows(fields, plane, part, field, place):
    start = ((plane * 2 + part) * fields + field) * planes + place
    return pl.ds(start, devices, stride=chunk_rows(fields))


def line_rows(fields, field, place):
    return pl.ds(field * planes + place, 2 * grid, stride=fields * planes)


def list_pairs(pairs_ref, order_ref):
    for index in range(pairs):
        order_ref[index] = 0
    count = jnp.int32(0)
    for index in range(pairs):
        order_ref[count] = index
        count += (pairs_ref[index // orbitals, index % orbitals] != 0).astype(jnp.int32)
    return count


def each_field(fields):
    def run(body):
        @pl.loop(0, fields // 4)
        def _(step):
            for index in range(4):
                body(4 * step + index)

        for field in range(fields - fields % 4, fields):
            body(field)

    return run


def partner_copies(band_ref, partners, occ_ref):
    return [
        (partner.at[0], occ_ref.at[band_ref[0] ^ other]) for other, partner in enumerate(partners)
    ]


def start_copies(copies, sem):
    copies = [
        pltpu.make_async_copy(source, target, sem.at[index])
        for index, (source, target) in enumerate(copies)
    ]
    for copy in copies:
        copy.start()
    return copies


def forward_kernel(fields, band_ref, pairs_ref, *refs):
    partners, refs = refs[:orbitals], refs[orbitals:]
    recv_any, z_any, y_any, out_ref, occ_ref, recv_ref, z_ref, y_ref, order_ref, sem = refs
    copies = start_copies(
        partner_copies(band_ref, partners, occ_ref)
        + [(recv_any, recv_ref), (z_any, z_ref), (y_any, y_ref)],
        sem,
    )
    list_pairs(pairs_ref, order_ref)
    for copy in copies:
        copy.wait()

    @each_field(fields)
    def _(field):
        couple = [order_ref[2 * field + part] for part in range(2)]
        value = jnp.concatenate(
            [
                jnp.concatenate(
                    [
                        recv_ref[pair // orbitals, plane] * occ_ref[pair % orbitals, plane]
                        for pair in couple
                    ],
                    1,
                )
                for plane in range(planes)
            ],
            0,
        )
        value = left_transform(y_ref, stack_parts(right_transform(value, z_ref)))
        for part in range(2):
            for place in range(planes):
                row = part * grid + place * devices
                for plane in range(planes):
                    out_ref[device_rows(fields, plane, part, field, place), :] = value[
                        row : row + devices, plane * grid : (plane + 1) * grid
                    ]


def filter_kernel(fields, spec_ref, coulomb_ref, x_ref, back_ref, out_ref):
    kernel = jnp.concatenate([coulomb_ref[:, place, :] for place in range(planes)], 1)
    kernel = jnp.concatenate([kernel, kernel], 0)

    @each_field(fields)
    def _(field):
        rows = [line_rows(fields, field, place) for place in range(planes)]
        value = jnp.concatenate([spec_ref[row, :] for row in rows], 1)
        value = left_transform(back_ref, left_transform(x_ref, value) * kernel)
        for place, row in enumerate(rows):
            out_ref[row, :] = value[:, place * grid : (place + 1) * grid]


def inverse_kernel(fields, band_ref, pairs_ref, weights_ref, *refs):
    partners, refs = refs[:orbitals], refs[orbitals:]
    spec_ref, y_ref, z_ref, out_ref, occ_ref, order_ref, sem = refs
    copies = start_copies(partner_copies(band_ref, partners, occ_ref), sem)
    count = list_pairs(pairs_ref, order_ref)
    out_ref[...] = jnp.zeros_like(out_ref)
    for copy in copies:
        copy.wait()

    @each_field(fields)
    def _(field):
        value = jnp.concatenate(
            [
                jnp.concatenate(
                    [
                        spec_ref[device_rows(fields, plane, part, field, place), :]
                        for plane in range(planes)
                    ],
                    1,
                )
                for part in range(2)
                for place in range(planes)
            ],
            0,
        )
        value = right_transform(stack_parts(left_transform(y_ref, value)), z_ref)
        for part in range(2):
            pair = order_ref[2 * field + part]
            received, occupied = pair // orbitals, pair % orbitals
            weight = jnp.where(2 * field + part < count, weights_ref[received, occupied], 0.0)
            for plane in range(planes):
                potential = value[
                    plane * grid : (plane + 1) * grid, part * grid : (part + 1) * grid
                ]
                out_ref[received, plane] += weight * occ_ref[occupied, plane] * potential


vmem = pl.BlockSpec(memory_space=pltpu.VMEM)
smem = pl.BlockSpec(memory_space=pltpu.SMEM)
anywhere = pl.BlockSpec(memory_space=pl.ANY)


def call(kernel, shape, in_specs, *operands, scratch=()):
    return pl.pallas_call(
        kernel,
        out_shape=jax.ShapeDtypeStruct(shape, jnp.float32),
        in_specs=in_specs,
        out_specs=vmem,
        scratch_shapes=scratch,
        compiler_params=pltpu.CompilerParams(vmem_limit_bytes=24 * 1024 * 1024),
    )(*operands)


def regroup(spectrum):
    return lax.all_to_all(
        spectrum.reshape(devices, -1, grid), "fft", split_axis=0, concat_axis=0, tiled=True
    ).reshape(spectrum.shape)


def neighbour(block, bits):
    return lax.ppermute(block, "band", [(index, index ^ bits) for index in range(orbitals)])


def exchange(fields, receiving, partners, coulomb, band, pair_list, weights, table):
    order = pltpu.SMEM((pairs,), jnp.int32)
    occupied = pltpu.VMEM((orbitals,) + partners[0].shape[1:], jnp.float32)
    spectrum = call(
        functools.partial(forward_kernel, fields),
        (devices * chunk_rows(fields), grid),
        [smem] * 2 + [anywhere] * (orbitals + 3),
        band,
        pair_list,
        *partners,
        receiving,
        table["z"],
        table["y"],
        scratch=[
            occupied,
            pltpu.VMEM(receiving.shape, jnp.float32),
            pltpu.VMEM(table["z"].shape, jnp.bfloat16),
            pltpu.VMEM(table["y"].shape, jnp.bfloat16),
            order,
            pltpu.SemaphoreType.DMA((orbitals + 3,)),
        ],
    )
    spectrum = regroup(spectrum)
    spectrum = call(
        functools.partial(filter_kernel, fields),
        spectrum.shape,
        [vmem] * 4,
        spectrum,
        coulomb,
        table["x"],
        table["x_back"],
    )
    spectrum = regroup(spectrum)
    return call(
        functools.partial(inverse_kernel, fields),
        receiving.shape,
        [smem] * 3 + [anywhere] * orbitals + [vmem] * 3,
        band,
        pair_list,
        weights,
        *partners,
        spectrum,
        table["y_back"],
        table["z_back"],
        scratch=[occupied, order, pltpu.SemaphoreType.DMA((orbitals,))],
    )


def on_device(receiving, occupied, coulomb, pair_list):
    far = neighbour(occupied, 2)
    partners = [occupied, neighbour(occupied, 1), far, neighbour(far, 1)]
    band = lax.axis_index("band").astype(jnp.int32).reshape(1)
    weights = pair_list.astype(jnp.float32) * (-mixing / grid**3)
    live = jnp.sum((pair_list != 0).astype(jnp.int32))
    chosen = jnp.maximum((live + 1) // 2 - field_counts[0], 0)
    return lax.switch(
        chosen,
        [functools.partial(exchange, fields) for fields in field_counts],
        receiving,
        partners,
        coulomb,
        band,
        pair_list,
        weights,
        lax.optimization_barrier(jax.tree.map(jnp.asarray, tables())),
    )


def solution(mesh):
    in_specs = (
        P("band", "fft", None, None),
        P("band", "fft", None, None),
        P(None, "fft", None),
        P("band", None),
    )
    out_specs = P("band", "fft", None, None)
    return jax.shard_map(
        on_device, mesh=mesh, in_specs=in_specs, out_specs=out_specs, check_vma=False
    )
```

```python
import functools

import numpy as np

import jax
import jax.numpy as jnp
from jax import lax
from jax.experimental import pallas as pl
from jax.experimental.pallas import tpu as pltpu
from jax.sharding import PartitionSpec as P

grid = 128
mixing = 0.25
devices = 64
planes = grid // devices
orbitals = 4
pairs = orbitals * orbitals
field_counts = (5, 6, 7, 8)


def halves(matrix):
    high = matrix.astype(jnp.bfloat16)
    low = (matrix - high.astype(np.float64)).astype(jnp.bfloat16)
    return np.stack([high, low])


def tables():
    angles = 2.0 * np.pi / grid * (np.arange(grid)[:, None] * np.arange(grid)[None, :] % grid)
    cos, sin = np.cos(angles), np.sin(angles)
    forward = np.block([[cos, -sin], [sin, cos]])
    inverse = np.block([[cos, sin], [-sin, cos]])
    part, row = np.divmod(np.arange(2 * grid), grid)
    spread = part * grid + row % devices * planes + row // devices
    woven = np.arange(2 * grid) % 2 * grid + np.arange(2 * grid) // 2
    return {
        "z": halves(forward),
        "y": halves(forward.T[spread]),
        "x": halves(forward.T[:, woven]),
        "x_back": halves(inverse.T[woven]),
        "y_back": halves(inverse.T[:, spread]),
        "z_back": halves(inverse),
    }


def split(value):
    high = value.astype(jnp.bfloat16)
    low = (value - high.astype(jnp.float32)).astype(jnp.bfloat16)
    return high, low


def dot(left, right):
    return jnp.dot(left, right, preferred_element_type=jnp.float32)


def right_transform(value, table):
    high, low = split(value)
    return dot(high, table[0]) + (dot(low, table[0]) + dot(high, table[1]))


def left_transform(table, value):
    high, low = split(value)
    return dot(table[0], high) + (dot(table[0], low) + dot(table[1], high))


def stack_parts(value):
    top, bottom = value[:grid], value[grid:]
    return jnp.concatenate(
        [
            jnp.concatenate([top[:, :grid], bottom[:, :grid]], 1),
            jnp.concatenate([top[:, grid:], bottom[:, grid:]], 1),
        ],
        0,
    )


def chunk_rows(fields):
    return planes * 2 * fields * planes


def device_rows(fields, plane, part, field, place):
    start = ((plane * 2 + part) * fields + field) * planes + place
    return pl.ds(start, devices, stride=chunk_rows(fields))


def line_rows(fields, field, place):
    return pl.ds(field * planes + place, 2 * grid, stride=fields * planes)


def list_pairs(pairs_ref, order_ref):
    for index in range(pairs):
        order_ref[index] = 0
    count = jnp.int32(0)
    for index in range(pairs):
        order_ref[count] = index
        count += (pairs_ref[index // orbitals, index % orbitals] != 0).astype(jnp.int32)
    return count


def each_field(fields):
    def run(body):
        @pl.loop(0, fields // 4)
        def _(step):
            for index in range(4):
                body(4 * step + index)

        for field in range(fields - fields % 4, fields):
            body(field)

    return run


def partner_copies(band_ref, partners, occ_ref):
    return [
        (partner.at[0], occ_ref.at[band_ref[0] ^ other]) for other, partner in enumerate(partners)
    ]


def start_copies(copies, sem):
    copies = [
        pltpu.make_async_copy(source, target, sem.at[index])
        for index, (source, target) in enumerate(copies)
    ]
    for copy in copies:
        copy.start()
    return copies


def forward_kernel(fields, band_ref, pairs_ref, *refs):
    partners, refs = refs[:orbitals], refs[orbitals:]
    recv_any, z_any, y_any, out_ref, occ_ref, recv_ref, z_ref, y_ref, order_ref, sem = refs
    copies = start_copies(
        partner_copies(band_ref, partners, occ_ref)
        + [(recv_any, recv_ref), (z_any, z_ref), (y_any, y_ref)],
        sem,
    )
    list_pairs(pairs_ref, order_ref)
    for copy in copies:
        copy.wait()

    @each_field(fields)
    def _(field):
        couple = [order_ref[2 * field + part] for part in range(2)]
        value = jnp.concatenate(
            [
                jnp.concatenate(
                    [
                        recv_ref[pair // orbitals, plane] * occ_ref[pair % orbitals, plane]
                        for pair in couple
                    ],
                    1,
                )
                for plane in range(planes)
            ],
            0,
        )
        value = left_transform(y_ref, stack_parts(right_transform(value, z_ref)))
        for part in range(2):
            for place in range(planes):
                row = part * grid + place * devices
                for plane in range(planes):
                    out_ref[device_rows(fields, plane, part, field, place), :] = value[
                        row : row + devices, plane * grid : (plane + 1) * grid
                    ]


def filter_kernel(fields, spec_ref, coulomb_ref, x_ref, back_ref, out_ref):
    kernel = jnp.concatenate([coulomb_ref[:, place, :] for place in range(planes)], 1)
    kernel = jnp.concatenate([kernel, kernel], 0)

    @each_field(fields)
    def _(field):
        rows = [line_rows(fields, field, place) for place in range(planes)]
        value = jnp.concatenate([spec_ref[row, :] for row in rows], 1)
        value = left_transform(back_ref, left_transform(x_ref, value) * kernel)
        for place, row in enumerate(rows):
            out_ref[row, :] = value[:, place * grid : (place + 1) * grid]


def inverse_kernel(fields, band_ref, pairs_ref, weights_ref, *refs):
    partners, refs = refs[:orbitals], refs[orbitals:]
    spec_ref, y_ref, z_ref, out_ref, occ_ref, order_ref, sem = refs
    copies = start_copies(partner_copies(band_ref, partners, occ_ref), sem)
    count = list_pairs(pairs_ref, order_ref)
    out_ref[...] = jnp.zeros_like(out_ref)
    for copy in copies:
        copy.wait()

    @each_field(fields)
    def _(field):
        value = jnp.concatenate(
            [
                jnp.concatenate(
                    [
                        spec_ref[device_rows(fields, plane, part, field, place), :]
                        for plane in range(planes)
                    ],
                    1,
                )
                for part in range(2)
                for place in range(planes)
            ],
            0,
        )
        value = right_transform(stack_parts(left_transform(y_ref, value)), z_ref)
        for part in range(2):
            pair = order_ref[2 * field + part]
            received, occupied = pair // orbitals, pair % orbitals
            weight = jnp.where(2 * field + part < count, weights_ref[received, occupied], 0.0)
            for plane in range(planes):
                potential = value[
                    plane * grid : (plane + 1) * grid, part * grid : (part + 1) * grid
                ]
                out_ref[received, plane] += weight * occ_ref[occupied, plane] * potential


vmem = pl.BlockSpec(memory_space=pltpu.VMEM)
smem = pl.BlockSpec(memory_space=pltpu.SMEM)
anywhere = pl.BlockSpec(memory_space=pl.ANY)


def call(kernel, shape, in_specs, *operands, scratch=()):
    return pl.pallas_call(
        kernel,
        out_shape=jax.ShapeDtypeStruct(shape, jnp.float32),
        in_specs=in_specs,
        out_specs=vmem,
        scratch_shapes=scratch,
        compiler_params=pltpu.CompilerParams(vmem_limit_bytes=24 * 1024 * 1024),
    )(*operands)


def regroup(spectrum):
    return lax.all_to_all(
        spectrum.reshape(devices, -1, grid), "fft", split_axis=0, concat_axis=0, tiled=True
    ).reshape(spectrum.shape)


def neighbour(block, bits):
    return lax.ppermute(block, "band", [(index, index ^ bits) for index in range(orbitals)])


def exchange(fields, receiving, partners, coulomb, band, pair_list, weights, table):
    order = pltpu.SMEM((pairs,), jnp.int32)
    occupied = pltpu.VMEM((orbitals,) + partners[0].shape[1:], jnp.float32)
    spectrum = call(
        functools.partial(forward_kernel, fields),
        (devices * chunk_rows(fields), grid),
        [smem] * 2 + [anywhere] * (orbitals + 3),
        band,
        pair_list,
        *partners,
        receiving,
        table["z"],
        table["y"],
        scratch=[
            occupied,
            pltpu.VMEM(receiving.shape, jnp.float32),
            pltpu.VMEM(table["z"].shape, jnp.bfloat16),
            pltpu.VMEM(table["y"].shape, jnp.bfloat16),
            order,
            pltpu.SemaphoreType.DMA((orbitals + 3,)),
        ],
    )
    spectrum = regroup(spectrum)
    spectrum = call(
        functools.partial(filter_kernel, fields),
        spectrum.shape,
        [vmem] * 4,
        spectrum,
        coulomb,
        table["x"],
        table["x_back"],
    )
    spectrum = regroup(spectrum)
    return call(
        functools.partial(inverse_kernel, fields),
        receiving.shape,
        [smem] * 3 + [anywhere] * orbitals + [vmem] * 3,
        band,
        pair_list,
        weights,
        *partners,
        spectrum,
        table["y_back"],
        table["z_back"],
        scratch=[occupied, order, pltpu.SemaphoreType.DMA((orbitals,))],
    )


def on_device(receiving, occupied, coulomb, pair_list):
    live = jnp.sum((pair_list != 0).astype(jnp.int32))
    chosen = jnp.maximum((live + 1) // 2 - field_counts[0], 0)
    far, chosen = lax.optimization_barrier((neighbour(occupied, 2), chosen))
    partners = [occupied, neighbour(occupied, 1), far, neighbour(far, 1)]
    band = lax.axis_index("band").astype(jnp.int32).reshape(1)
    weights = pair_list.astype(jnp.float32) * (-mixing / grid**3)
    return lax.switch(
        chosen,
        [functools.partial(exchange, fields) for fields in field_counts],
        receiving,
        partners,
        coulomb,
        band,
        pair_list,
        weights,
        lax.optimization_barrier(jax.tree.map(jnp.asarray, tables())),
    )


def solution(mesh):
    in_specs = (
        P("band", "fft", None, None),
        P("band", "fft", None, None),
        P(None, "fft", None),
        P("band", None),
    )
    out_specs = P("band", "fft", None, None)
    return jax.shard_map(
        on_device, mesh=mesh, in_specs=in_specs, out_specs=out_specs, check_vma=False
    )
```

```python
import functools

import numpy as np

import jax
import jax.numpy as jnp
from jax import lax
from jax.experimental import pallas as pl
from jax.experimental.pallas import tpu as pltpu
from jax.sharding import PartitionSpec as P

grid = 128
mixing = 0.25
devices = 64
planes = grid // devices
orbitals = 4
pairs = orbitals * orbitals
field_counts = (5, 6, 7, 8)


def halves(matrix):
    high = matrix.astype(jnp.bfloat16)
    low = (matrix - high.astype(np.float64)).astype(jnp.bfloat16)
    return np.stack([high, low])


def tables():
    angles = 2.0 * np.pi / grid * (np.arange(grid)[:, None] * np.arange(grid)[None, :] % grid)
    cos, sin = np.cos(angles), np.sin(angles)
    forward = np.block([[cos, -sin], [sin, cos]])
    inverse = np.block([[cos, sin], [-sin, cos]])
    part, row = np.divmod(np.arange(2 * grid), grid)
    spread = part * grid + row % devices * planes + row // devices
    woven = np.arange(2 * grid) % 2 * grid + np.arange(2 * grid) // 2
    return {
        "z": halves(forward),
        "y": halves(forward.T[spread]),
        "x": halves(forward.T[:, woven]),
        "x_back": halves(inverse.T[woven]),
        "y_back": halves(inverse.T[:, spread]),
        "z_back": halves(inverse),
    }


def split(value):
    high = value.astype(jnp.bfloat16)
    low = (value - high.astype(jnp.float32)).astype(jnp.bfloat16)
    return high, low


def dot(left, right):
    return jnp.dot(left, right, preferred_element_type=jnp.float32)


def right_transform(value, table):
    high, low = split(value)
    return dot(high, table[0]) + (dot(low, table[0]) + dot(high, table[1]))


def left_transform(table, value):
    high, low = split(value)
    return dot(table[0], high) + (dot(table[0], low) + dot(table[1], high))


def stack_parts(value):
    top, bottom = value[:grid], value[grid:]
    return jnp.concatenate(
        [
            jnp.concatenate([top[:, :grid], bottom[:, :grid]], 1),
            jnp.concatenate([top[:, grid:], bottom[:, grid:]], 1),
        ],
        0,
    )


def chunk_rows(fields):
    return planes * 2 * fields * planes


def device_rows(fields, plane, part, field, place):
    start = ((plane * 2 + part) * fields + field) * planes + place
    return pl.ds(start, devices, stride=chunk_rows(fields))


def line_rows(fields, field, place):
    return pl.ds(field * planes + place, 2 * grid, stride=fields * planes)


def list_pairs(pairs_ref, order_ref):
    for index in range(pairs):
        order_ref[index] = 0
    count = jnp.int32(0)
    for index in range(pairs):
        order_ref[count] = index
        count += (pairs_ref[index // orbitals, index % orbitals] != 0).astype(jnp.int32)
    return count


def each_field(fields):
    def run(body):
        @pl.loop(0, fields // 4)
        def _(step):
            for index in range(4):
                body(4 * step + index)

        for field in range(fields - fields % 4, fields):
            body(field)

    return run


def partner_copies(band_ref, partners, occ_ref):
    return [
        (partner.at[0], occ_ref.at[band_ref[0] ^ other]) for other, partner in enumerate(partners)
    ]


def start_copies(copies, sem):
    copies = [
        pltpu.make_async_copy(source, target, sem.at[index])
        for index, (source, target) in enumerate(copies)
    ]
    for copy in copies:
        copy.start()
    return copies


def forward_kernel(fields, band_ref, pairs_ref, *refs):
    partners, refs = refs[:orbitals], refs[orbitals:]
    recv_any, z_any, y_any, out_ref, occ_ref, recv_ref, z_ref, y_ref, order_ref, sem = refs
    copies = start_copies(
        partner_copies(band_ref, partners, occ_ref)
        + [(recv_any, recv_ref), (z_any, z_ref), (y_any, y_ref)],
        sem,
    )
    list_pairs(pairs_ref, order_ref)
    for copy in copies:
        copy.wait()

    @each_field(fields)
    def _(field):
        couple = [order_ref[2 * field + part] for part in range(2)]
        value = jnp.concatenate(
            [
                jnp.concatenate(
                    [
                        recv_ref[pair // orbitals, plane] * occ_ref[pair % orbitals, plane]
                        for pair in couple
                    ],
                    1,
                )
                for plane in range(planes)
            ],
            0,
        )
        value = left_transform(y_ref, stack_parts(right_transform(value, z_ref)))
        for part in range(2):
            for place in range(planes):
                row = part * grid + place * devices
                for plane in range(planes):
                    out_ref[device_rows(fields, plane, part, field, place), :] = value[
                        row : row + devices, plane * grid : (plane + 1) * grid
                    ]


def filter_kernel(fields, spec_ref, coulomb_ref, x_ref, back_ref, out_ref):
    kernel = jnp.concatenate([coulomb_ref[:, place, :] for place in range(planes)], 1)
    kernel = jnp.concatenate([kernel, kernel], 0)

    @each_field(fields)
    def _(field):
        rows = [line_rows(fields, field, place) for place in range(planes)]
        value = jnp.concatenate([spec_ref[row, :] for row in rows], 1)
        value = left_transform(back_ref, left_transform(x_ref, value) * kernel)
        for place, row in enumerate(rows):
            out_ref[row, :] = value[:, place * grid : (place + 1) * grid]


def inverse_kernel(fields, band_ref, pairs_ref, weights_ref, *refs):
    partners, refs = refs[:orbitals], refs[orbitals:]
    spec_ref, y_ref, z_ref, out_ref, occ_ref, order_ref = refs
    for other, partner in enumerate(partners):
        occ_ref[band_ref[0] ^ other] = partner[0]
    count = list_pairs(pairs_ref, order_ref)
    out_ref[...] = jnp.zeros_like(out_ref)

    @each_field(fields)
    def _(field):
        value = jnp.concatenate(
            [
                jnp.concatenate(
                    [
                        spec_ref[device_rows(fields, plane, part, field, place), :]
                        for plane in range(planes)
                    ],
                    1,
                )
                for part in range(2)
                for place in range(planes)
            ],
            0,
        )
        value = right_transform(stack_parts(left_transform(y_ref, value)), z_ref)
        for part in range(2):
            pair = order_ref[2 * field + part]
            received, occupied = pair // orbitals, pair % orbitals
            weight = jnp.where(2 * field + part < count, weights_ref[received, occupied], 0.0)
            for plane in range(planes):
                potential = value[
                    plane * grid : (plane + 1) * grid, part * grid : (part + 1) * grid
                ]
                out_ref[received, plane] += weight * occ_ref[occupied, plane] * potential


vmem = pl.BlockSpec(memory_space=pltpu.VMEM)
smem = pl.BlockSpec(memory_space=pltpu.SMEM)
anywhere = pl.BlockSpec(memory_space=pl.ANY)


def call(kernel, shape, in_specs, *operands, scratch=()):
    return pl.pallas_call(
        kernel,
        out_shape=jax.ShapeDtypeStruct(shape, jnp.float32),
        in_specs=in_specs,
        out_specs=vmem,
        scratch_shapes=scratch,
        compiler_params=pltpu.CompilerParams(vmem_limit_bytes=24 * 1024 * 1024),
    )(*operands)


def regroup(spectrum):
    return lax.all_to_all(
        spectrum.reshape(devices, -1, grid), "fft", split_axis=0, concat_axis=0, tiled=True
    ).reshape(spectrum.shape)


def neighbour(block, bits):
    return lax.ppermute(block, "band", [(index, index ^ bits) for index in range(orbitals)])


def exchange(fields, receiving, partners, coulomb, band, pair_list, weights, table):
    order = pltpu.SMEM((pairs,), jnp.int32)
    occupied = pltpu.VMEM((orbitals,) + partners[0].shape[1:], jnp.float32)
    spectrum = call(
        functools.partial(forward_kernel, fields),
        (devices * chunk_rows(fields), grid),
        [smem] * 2 + [anywhere] * (orbitals + 3),
        band,
        pair_list,
        *partners,
        receiving,
        table["z"],
        table["y"],
        scratch=[
            occupied,
            pltpu.VMEM(receiving.shape, jnp.float32),
            pltpu.VMEM(table["z"].shape, jnp.bfloat16),
            pltpu.VMEM(table["y"].shape, jnp.bfloat16),
            order,
            pltpu.SemaphoreType.DMA((orbitals + 3,)),
        ],
    )
    spectrum = regroup(spectrum)
    spectrum = call(
        functools.partial(filter_kernel, fields),
        spectrum.shape,
        [vmem] * 4,
        spectrum,
        coulomb,
        table["x"],
        table["x_back"],
    )
    spectrum = regroup(spectrum)
    return call(
        functools.partial(inverse_kernel, fields),
        receiving.shape,
        [smem] * 3 + [vmem] * (orbitals + 3),
        band,
        pair_list,
        weights,
        *partners,
        spectrum,
        table["y_back"],
        table["z_back"],
        scratch=[occupied, order],
    )


def on_device(receiving, occupied, coulomb, pair_list):
    live = jnp.sum((pair_list != 0).astype(jnp.int32))
    chosen = jnp.maximum((live + 1) // 2 - field_counts[0], 0)
    far, chosen = lax.optimization_barrier((neighbour(occupied, 2), chosen))
    partners = [occupied, neighbour(occupied, 1), far, neighbour(far, 1)]
    band = lax.axis_index("band").astype(jnp.int32).reshape(1)
    weights = pair_list.astype(jnp.float32) * (-mixing / grid**3)
    return lax.switch(
        chosen,
        [functools.partial(exchange, fields) for fields in field_counts],
        receiving,
        partners,
        coulomb,
        band,
        pair_list,
        weights,
        lax.optimization_barrier(jax.tree.map(jnp.asarray, tables())),
    )


def solution(mesh):
    in_specs = (
        P("band", "fft", None, None),
        P("band", "fft", None, None),
        P(None, "fft", None),
        P("band", None),
    )
    out_specs = P("band", "fft", None, None)
    return jax.shard_map(
        on_device, mesh=mesh, in_specs=in_specs, out_specs=out_specs, check_vma=False
    )
```

```python
import functools

import numpy as np

import jax
import jax.numpy as jnp
from jax import lax
from jax.experimental import pallas as pl
from jax.experimental.pallas import tpu as pltpu
from jax.sharding import PartitionSpec as P

grid = 128
mixing = 0.25
devices = 64
planes = grid // devices
orbitals = 4
pairs = orbitals * orbitals
field_counts = (5, 6, 7, 8)


def halves(matrix):
    high = matrix.astype(jnp.bfloat16)
    low = (matrix - high.astype(np.float64)).astype(jnp.bfloat16)
    return np.stack([high, low])


def tables():
    angles = 2.0 * np.pi / grid * (np.arange(grid)[:, None] * np.arange(grid)[None, :] % grid)
    cos, sin = np.cos(angles), np.sin(angles)
    forward = np.block([[cos, -sin], [sin, cos]])
    inverse = np.block([[cos, sin], [-sin, cos]])
    part, row = np.divmod(np.arange(2 * grid), grid)
    spread = part * grid + row % devices * planes + row // devices
    woven = np.arange(2 * grid) % 2 * grid + np.arange(2 * grid) // 2
    return {
        "z": halves(forward),
        "y": halves(forward.T[spread]),
        "x": halves(forward.T[:, woven]),
        "x_back": halves(inverse.T[woven]),
        "y_back": halves(inverse.T[:, spread]),
        "z_back": halves(inverse),
    }


def split(value):
    high = value.astype(jnp.bfloat16)
    low = (value - high.astype(jnp.float32)).astype(jnp.bfloat16)
    return high, low


def dot(left, right):
    return jnp.dot(left, right, preferred_element_type=jnp.float32)


def right_transform(value, table):
    high, low = split(value)
    return dot(high, table[0]) + (dot(low, table[0]) + dot(high, table[1]))


def left_transform(table, value):
    high, low = split(value)
    return dot(table[0], high) + (dot(table[0], low) + dot(table[1], high))


def stack_parts(value):
    top, bottom = value[:grid], value[grid:]
    return jnp.concatenate(
        [
            jnp.concatenate([top[:, :grid], bottom[:, :grid]], 1),
            jnp.concatenate([top[:, grid:], bottom[:, grid:]], 1),
        ],
        0,
    )


def chunk_rows(fields):
    return planes * 2 * fields * planes


def device_rows(fields, plane, part, field, place):
    start = ((plane * 2 + part) * fields + field) * planes + place
    return pl.ds(start, devices, stride=chunk_rows(fields))


def line_rows(fields, field, place):
    return pl.ds(field * planes + place, 2 * grid, stride=fields * planes)


def list_pairs(pairs_ref, order_ref):
    for index in range(pairs):
        order_ref[index] = 0
    count = jnp.int32(0)
    for index in range(pairs):
        order_ref[count] = index
        count += (pairs_ref[index // orbitals, index % orbitals] != 0).astype(jnp.int32)
    return count


def each_field(fields):
    def run(body):
        for field in range(fields):
            body(field)

    return run


def partner_copies(band_ref, partners, occ_ref):
    return [
        (partner.at[0], occ_ref.at[band_ref[0] ^ other]) for other, partner in enumerate(partners)
    ]


def start_copies(copies, sem):
    copies = [
        pltpu.make_async_copy(source, target, sem.at[index])
        for index, (source, target) in enumerate(copies)
    ]
    for copy in copies:
        copy.start()
    return copies


def forward_kernel(fields, band_ref, pairs_ref, *refs):
    partners, refs = refs[:orbitals], refs[orbitals:]
    recv_any, z_any, y_any, out_ref, occ_ref, recv_ref, z_ref, y_ref, order_ref, sem = refs
    copies = start_copies(
        partner_copies(band_ref, partners, occ_ref)
        + [(recv_any, recv_ref), (z_any, z_ref), (y_any, y_ref)],
        sem,
    )
    list_pairs(pairs_ref, order_ref)
    for copy in copies:
        copy.wait()

    @each_field(fields)
    def _(field):
        couple = [order_ref[2 * field + part] for part in range(2)]
        value = jnp.concatenate(
            [
                jnp.concatenate(
                    [
                        recv_ref[pair // orbitals, plane] * occ_ref[pair % orbitals, plane]
                        for pair in couple
                    ],
                    1,
                )
                for plane in range(planes)
            ],
            0,
        )
        value = left_transform(y_ref, stack_parts(right_transform(value, z_ref)))
        for part in range(2):
            for place in range(planes):
                row = part * grid + place * devices
                for plane in range(planes):
                    out_ref[device_rows(fields, plane, part, field, place), :] = value[
                        row : row + devices, plane * grid : (plane + 1) * grid
                    ]


def filter_kernel(fields, spec_ref, coulomb_ref, x_ref, back_ref, out_ref):
    kernel = jnp.concatenate([coulomb_ref[:, place, :] for place in range(planes)], 1)
    kernel = jnp.concatenate([kernel, kernel], 0)

    @each_field(fields)
    def _(field):
        rows = [line_rows(fields, field, place) for place in range(planes)]
        value = jnp.concatenate([spec_ref[row, :] for row in rows], 1)
        value = left_transform(back_ref, left_transform(x_ref, value) * kernel)
        for place, row in enumerate(rows):
            out_ref[row, :] = value[:, place * grid : (place + 1) * grid]


def inverse_kernel(fields, band_ref, pairs_ref, weights_ref, *refs):
    partners, refs = refs[:orbitals], refs[orbitals:]
    spec_ref, y_ref, z_ref, out_ref, occ_ref, order_ref = refs
    for other, partner in enumerate(partners):
        occ_ref[band_ref[0] ^ other] = partner[0]
    count = list_pairs(pairs_ref, order_ref)
    out_ref[...] = jnp.zeros_like(out_ref)

    @each_field(fields)
    def _(field):
        value = jnp.concatenate(
            [
                jnp.concatenate(
                    [
                        spec_ref[device_rows(fields, plane, part, field, place), :]
                        for plane in range(planes)
                    ],
                    1,
                )
                for part in range(2)
                for place in range(planes)
            ],
            0,
        )
        value = right_transform(stack_parts(left_transform(y_ref, value)), z_ref)
        for part in range(2):
            pair = order_ref[2 * field + part]
            received, occupied = pair // orbitals, pair % orbitals
            weight = jnp.where(2 * field + part < count, weights_ref[received, occupied], 0.0)
            for plane in range(planes):
                potential = value[
                    plane * grid : (plane + 1) * grid, part * grid : (part + 1) * grid
                ]
                out_ref[received, plane] += weight * occ_ref[occupied, plane] * potential


vmem = pl.BlockSpec(memory_space=pltpu.VMEM)
smem = pl.BlockSpec(memory_space=pltpu.SMEM)
anywhere = pl.BlockSpec(memory_space=pl.ANY)


def call(kernel, shape, in_specs, *operands, scratch=()):
    return pl.pallas_call(
        kernel,
        out_shape=jax.ShapeDtypeStruct(shape, jnp.float32),
        in_specs=in_specs,
        out_specs=vmem,
        scratch_shapes=scratch,
        compiler_params=pltpu.CompilerParams(vmem_limit_bytes=24 * 1024 * 1024),
    )(*operands)


def regroup(spectrum):
    return lax.all_to_all(
        spectrum.reshape(devices, -1, grid), "fft", split_axis=0, concat_axis=0, tiled=True
    ).reshape(spectrum.shape)


def neighbour(block, bits):
    return lax.ppermute(block, "band", [(index, index ^ bits) for index in range(orbitals)])


def exchange(fields, receiving, partners, coulomb, band, pair_list, weights, table):
    order = pltpu.SMEM((pairs,), jnp.int32)
    occupied = pltpu.VMEM((orbitals,) + partners[0].shape[1:], jnp.float32)
    spectrum = call(
        functools.partial(forward_kernel, fields),
        (devices * chunk_rows(fields), grid),
        [smem] * 2 + [anywhere] * (orbitals + 3),
        band,
        pair_list,
        *partners,
        receiving,
        table["z"],
        table["y"],
        scratch=[
            occupied,
            pltpu.VMEM(receiving.shape, jnp.float32),
            pltpu.VMEM(table["z"].shape, jnp.bfloat16),
            pltpu.VMEM(table["y"].shape, jnp.bfloat16),
            order,
            pltpu.SemaphoreType.DMA((orbitals + 3,)),
        ],
    )
    spectrum = regroup(spectrum)
    spectrum = call(
        functools.partial(filter_kernel, fields),
        spectrum.shape,
        [vmem] * 4,
        spectrum,
        coulomb,
        table["x"],
        table["x_back"],
    )
    spectrum = regroup(spectrum)
    return call(
        functools.partial(inverse_kernel, fields),
        receiving.shape,
        [smem] * 3 + [vmem] * (orbitals + 3),
        band,
        pair_list,
        weights,
        *partners,
        spectrum,
        table["y_back"],
        table["z_back"],
        scratch=[occupied, order],
    )


def on_device(receiving, occupied, coulomb, pair_list):
    live = jnp.sum((pair_list != 0).astype(jnp.int32))
    chosen = jnp.maximum((live + 1) // 2 - field_counts[0], 0)
    far, chosen = lax.optimization_barrier((neighbour(occupied, 2), chosen))
    partners = [occupied, neighbour(occupied, 1), far, neighbour(far, 1)]
    band = lax.axis_index("band").astype(jnp.int32).reshape(1)
    weights = pair_list.astype(jnp.float32) * (-mixing / grid**3)
    return lax.switch(
        chosen,
        [functools.partial(exchange, fields) for fields in field_counts],
        receiving,
        partners,
        coulomb,
        band,
        pair_list,
        weights,
        lax.optimization_barrier(jax.tree.map(jnp.asarray, tables())),
    )


def solution(mesh):
    in_specs = (
        P("band", "fft", None, None),
        P("band", "fft", None, None),
        P(None, "fft", None),
        P("band", None),
    )
    out_specs = P("band", "fft", None, None)
    return jax.shard_map(
        on_device, mesh=mesh, in_specs=in_specs, out_specs=out_specs, check_vma=False
    )
```
